256 devices in a mesh: rad: 16 (over x_lo, y, core), mode: 16 (over x_hi, z).
Axes of the slice: x: 4 (x_hi: 2, x_lo: 2; x = x_hi * 2 + x_lo), y: 4, z: 8, core: 2. Of those that a mesh axis runs over, the one named last changes fastest.
Arguments:
- field_state: float32 [2, 640, 262144], P(None, 'rad', 'mode'), may hold values from -6 to 6
- forcing: bfloat16 [2, 640, 262144], P(None, 'rad', 'mode'), may hold values from -6 to 6
- inverses: bfloat16 [2, 256, 640, 640], P(None, ('rad', 'mode')), may hold values from -1 to 2
- owned_degree: int32 [256], P(('rad', 'mode')), may hold values from 0 to 767
Outputs:
- section_fields: bfloat16 [2, 640, 262144], P(None, 'rad', 'mode')
The draws below stay inside these ranges and needn't reach their ends.
All inputs are finite; a program needn't handle non-finite values.
Results may differ from the reference program's by a relative error of at most 0.0049.
Values may be sent and summed in bfloat16 or wider, within the bound.
No kernel may reach another device: no remote copies, remote signals or barrier semaphores. Data moves between devices by JAX's collectives and lax.ppermute only.
A program may use at most 128 MiB of HBM per device.

```python
import jax
import jax.numpy as jnp
from jax import lax

NR = 640
LMAX = 768
CD = 1024
SLOTS = 256
NCOL = 262144
N_MODE = 16


def draw_inverses(key, part):
    key = jax.random.fold_in(key, 7)
    key_diag = jax.random.fold_in(key, 1)
    key_off = jax.random.fold_in(key, 2)
    diagonal = jnp.exp(jax.random.uniform(key_diag, (2, SLOTS, NR), jnp.float32, jnp.log(0.4), jnp.log(1.2)))
    spread = jax.random.truncated_normal(key_off, -4.0, 4.0, (2, SLOTS, NR, NR), jnp.float32)
    off_part = spread * (0.5 / NR ** 0.5)
    identity = jnp.eye(NR, dtype=jnp.float32)
    return (off_part + identity[None, None] * diagonal[..., None]).astype(jnp.bfloat16)


def touch_ends(entries, rng, smallest, high):
    index_at = [jax.random.randint(jax.random.fold_in(rng, axis), (), 0, length) for axis, length in enumerate(entries.shape)]
    longest = entries.shape.index(max(entries.shape))
    next_to = index_at[:longest] + [(index_at[longest] + 1) % entries.shape[longest]] + index_at[longest + 1:]
    return entries.at[tuple(index_at)].set(smallest).at[tuple(next_to)].set(high)


def shard_levels(rng, extent, cuts, smallest, largest):
    def one(position, shards_of):
        steps = jax.random.uniform(jax.random.fold_in(jax.random.fold_in(rng, 6), position), (shards_of,), jnp.float32, smallest / len(cuts), largest / len(cuts))
        return jnp.repeat(jnp.exp(steps), extent[position] // shards_of).reshape((-1,) + (1,) * (len(extent) - position - 1))

    gain = one(*cuts[0])
    for cut in cuts[1:]:
        gain = gain * one(*cut)
    return gain


def bell_draw(stream_key, extent, width, reach, pieces=(), kind=jnp.bfloat16):
    entries = jax.random.normal(stream_key, extent, jnp.float32) * width
    if len(pieces) > 0:
        entries = shard_levels(stream_key, extent, pieces, -0.22, 0.18) * entries
    return jnp.clip(entries, min=-reach, max=reach).astype(kind)


def setup_inputs(seed: int = 0) -> dict:
    keys = jax.random.split(jax.random.key(seed), 5)
    return {
        "field_state": bell_draw(keys[0], (2, NR, NCOL), 1.0, 6.0, ((1, 16), (2, 16)), jnp.float32),
        "forcing": bell_draw(keys[1], (2, NR, NCOL), 1.0, 6.0, ((1, 16), (2, 16))),
        "inverses": draw_inverses(jax.random.fold_in(keys[4], 71), 0),
        "owned_degree": touch_ends(jax.random.randint(keys[3], (SLOTS,), 0, LMAX), jax.random.fold_in(keys[3], 1), 0, LMAX - 1).astype(jnp.int32),
    }


R_INNER = 0.35
R_OUTER = 1.0
EXPLICIT_WEIGHT = (0.45, 0.35)
FORCING_STEP = 0.5


def explicit_update(values, forcing, below, above, radius_grid, degree_term, spacing):
    weights = jnp.array(EXPLICIT_WEIGHT, jnp.float32)[:, None, None]
    ratio = (spacing / radius_grid)[None, :, None]
    second = above - 2.0 * values + below
    slope = ratio * (above - below)
    horizontal = (spacing * spacing) * degree_term[None, None, :] / (radius_grid * radius_grid)[None, :, None] * values
    return values + FORCING_STEP * forcing.astype(jnp.float32) + weights * (second + slope - horizontal)


def reference(field_state, forcing, inverses, owned_degree):
    spacing = (R_OUTER - R_INNER) / (NR - 1)
    radius_grid = R_INNER + spacing * jnp.arange(NR, dtype=jnp.int32).astype(jnp.float32)
    piece_width = CD // N_MODE
    state_view = field_state.reshape(2, NR, N_MODE, SLOTS, piece_width)
    forcing_view = forcing.reshape(2, NR, N_MODE, SLOTS, piece_width)

    def per_owner(owner):
        column_state = lax.dynamic_index_in_dim(state_view, owner, 3, keepdims=False).reshape(2, NR, CD)
        column_forcing = lax.dynamic_index_in_dim(forcing_view, owner, 3, keepdims=False).reshape(2, NR, CD)
        inverse_pair = lax.dynamic_index_in_dim(inverses, owner, 1, keepdims=False)
        degree = lax.dynamic_index_in_dim(owned_degree, owner, 0, keepdims=True).astype(jnp.float32)
        degree_term = degree * (degree + 1.0)
        zero_row = jnp.zeros((2, 1, CD), jnp.float32)
        below = jnp.concatenate([zero_row, column_state[:, :-1]], axis=1)
        above = jnp.concatenate([column_state[:, 1:], zero_row], axis=1)
        right_side = explicit_update(column_state, column_forcing, below, above, radius_grid, degree_term, spacing).astype(jnp.bfloat16)
        solved = jnp.einsum("fij,fjc->fic", inverse_pair.astype(jnp.float32), right_side.astype(jnp.float32))
        return solved.astype(jnp.bfloat16)

    blocks = lax.map(per_owner, jnp.arange(SLOTS, dtype=jnp.int32))
    blocks = blocks.reshape(SLOTS, 2, NR, N_MODE, piece_width)
    assembled = jnp.transpose(blocks, (1, 2, 3, 0, 4)).reshape(2, NR, NCOL)
    return assembled
```

```python
import functools

import jax
import jax.numpy as jnp
from jax import lax
from jax.experimental import pallas as pl
from jax.experimental.pallas import tpu as pltpu
from jax.sharding import PartitionSpec as P

R_INNER = 0.35
R_OUTER = 1.0
EXPLICIT_WEIGHT = (0.45, 0.35)
FORCING_STEP = 0.5
AXES = ("rad", "mode")
LANES = 128


def pair_lanes(first, second, low):
    mixed = pltpu.roll(jnp.where(low, second, first), LANES // 2, axis=1)
    return jnp.where(low, first, mixed), jnp.where(low, mixed, second)


def right_side_kernel(spacing, piece, degree_ref, up_ref, down_ref, state_ref, forcing_ref, out_ref):
    rows, cols = state_ref.shape[1:]
    start = pl.program_id(0) * (cols // piece)
    row = lax.broadcasted_iota(jnp.int32, (rows, LANES), 0)
    low = lax.broadcasted_iota(jnp.int32, (rows, LANES), 1) < piece
    first_row, last_row = row == 0, row == rows - 1
    radius = R_INNER + spacing * (lax.axis_index("rad") * rows + row).astype(jnp.float32)
    ratio = spacing / radius
    square = (spacing * spacing) / (radius * radius)
    for j in range(cols // LANES):
        lanes = slice(j * LANES, (j + 1) * LANES)
        even = degree_ref[start + 2 * j]
        odd = degree_ref[start + 2 * j + 1]
        degree_term = jnp.where(low, even * (even + 1.0), odd * (odd + 1.0))
        horizontal = square * degree_term
        sides = []
        for f, weight in enumerate(EXPLICIT_WEIGHT):
            values = state_ref[f, :, lanes]
            above = jnp.where(last_row, up_ref[f, :, lanes], pltpu.roll(values, rows - 1, axis=0))
            below = jnp.where(first_row, down_ref[f, :, lanes], pltpu.roll(values, 1, axis=0))
            sides.append(
                values
                + FORCING_STEP * forcing_ref[f, :, lanes].astype(jnp.float32)
                + weight
                * ((above - 2.0 * values + below) + ratio * (above - below) - horizontal * values)
            )
        first, second = pair_lanes(sides[0], sides[1], low)
        out_ref[2 * j] = first.astype(jnp.bfloat16)
        out_ref[2 * j + 1] = second.astype(jnp.bfloat16)


def solve_kernel(piece, inverse_ref, side_ref, out_ref):
    senders, groups, rows, _ = side_ref.shape
    whole = senders * rows
    sides = [
        side_ref[:, g].astype(jnp.float32).reshape(whole, LANES).astype(jnp.bfloat16)
        for g in range(groups)
    ]
    side = jnp.concatenate(sides, axis=1)
    low = lax.broadcasted_iota(jnp.int32, (whole, groups * LANES), 1) % LANES < piece
    solved = jnp.where(
        low,
        jnp.dot(inverse_ref[0, 0], side, preferred_element_type=jnp.float32),
        jnp.dot(inverse_ref[1, 0], side, preferred_element_type=jnp.float32),
    )
    for g in range(groups):
        out_ref[:, g] = (
            solved[:, g * LANES : (g + 1) * LANES]
            .reshape(senders, rows, LANES)
            .astype(jnp.bfloat16)
        )


def unpack_kernel(piece, solved_ref, out_ref):
    owners, rows, _ = solved_ref.shape
    low = lax.broadcasted_iota(jnp.int32, (rows, LANES), 1) < piece
    for j in range(owners // 2):
        lanes = slice(j * LANES, (j + 1) * LANES)
        first, second = pair_lanes(
            solved_ref[2 * j].astype(jnp.float32), solved_ref[2 * j + 1].astype(jnp.float32), low
        )
        out_ref[0, :, lanes] = first.astype(jnp.bfloat16)
        out_ref[1, :, lanes] = second.astype(jnp.bfloat16)


def body(field_state, forcing, inverses, owned_degree):
    fields, rows, group_cols = field_state.shape
    rad_count = lax.axis_size("rad")
    mode_count = lax.axis_size("mode")
    slots = rad_count * mode_count
    whole_rows = rows * rad_count
    piece = group_cols // slots
    spacing = (R_OUTER - R_INNER) / (whole_rows - 1)

    degrees = lax.all_to_all(
        jnp.broadcast_to(owned_degree.astype(jnp.float32), (slots,)), AXES, 0, 0, tiled=True
    )
    from_above = lax.ppermute(
        field_state[:, :1], "rad", [(i + 1, i) for i in range(rad_count - 1)]
    )
    from_below = lax.ppermute(
        field_state[:, rows - 1 :], "rad", [(i, i + 1) for i in range(rad_count - 1)]
    )

    cols = 2048
    packed = pl.pallas_call(
        functools.partial(right_side_kernel, spacing, piece),
        grid=(group_cols // cols,),
        in_specs=[
            pl.BlockSpec(memory_space=pltpu.SMEM),
            pl.BlockSpec((fields, 1, cols), lambda i: (0, 0, i)),
            pl.BlockSpec((fields, 1, cols), lambda i: (0, 0, i)),
            pl.BlockSpec((fields, rows, cols), lambda i: (0, 0, i)),
            pl.BlockSpec((fields, rows, cols), lambda i: (0, 0, i)),
        ],
        out_specs=pl.BlockSpec((cols // piece, rows, LANES), lambda i: (i, 0, 0)),
        out_shape=jax.ShapeDtypeStruct((slots, rows, LANES), jnp.bfloat16),
        name="right_side",
    )(degrees, from_above, from_below, field_state, forcing)

    packed = lax.all_to_all(packed, AXES, 0, 0, tiled=True)

    groups = 4
    solved = pl.pallas_call(
        functools.partial(solve_kernel, piece),
        grid=(mode_count // groups,),
        in_specs=[
            pl.BlockSpec((fields, 1, whole_rows, whole_rows), lambda i: (0, 0, 0, 0)),
            pl.BlockSpec((rad_count, groups, rows, LANES), lambda i: (0, i, 0, 0)),
        ],
        out_specs=pl.BlockSpec((rad_count, groups, rows, LANES), lambda i: (0, i, 0, 0)),
        out_shape=jax.ShapeDtypeStruct((rad_count, mode_count, rows, LANES), jnp.bfloat16),
        compiler_params=pltpu.CompilerParams(vmem_limit_bytes=48 * 1024 * 1024),
        name="solve",
    )(inverses, packed.reshape(rad_count, mode_count, rows, LANES))

    solved = lax.all_to_all(solved.reshape(slots, rows, LANES), AXES, 0, 0, tiled=True)

    owners = 32
    return pl.pallas_call(
        functools.partial(unpack_kernel, piece),
        grid=(slots // owners,),
        in_specs=[pl.BlockSpec((owners, rows, LANES), lambda i: (i, 0, 0))],
        out_specs=pl.BlockSpec((fields, rows, owners * piece), lambda i: (0, 0, i)),
        out_shape=jax.ShapeDtypeStruct((fields, rows, group_cols), jnp.bfloat16),
        name="unpack",
    )(solved)


def solution(mesh):
    in_specs = (
        P(None, "rad", "mode"),
        P(None, "rad", "mode"),
        P(None, ("rad", "mode"), None, None),
        P(("rad", "mode")),
    )
    out_specs = P(None, "rad", "mode")
    return jax.shard_map(body, mesh=mesh, in_specs=in_specs, out_specs=out_specs, check_vma=False)
```

```python
import functools

import jax
import jax.numpy as jnp
from jax import lax
from jax.experimental import pallas as pl
from jax.experimental.pallas import tpu as pltpu
from jax.sharding import PartitionSpec as P

R_INNER = 0.35
R_OUTER = 1.0
EXPLICIT_WEIGHT = (0.45, 0.35)
FORCING_STEP = 0.5
AXES = ("rad", "mode")
LANES = 128
CORES = 2
DEPTH = 8
QUAD = DEPTH // 2
SMALL_VMEM = 24 * 1024 * 1024
LARGE_VMEM = 56 * 1024 * 1024


def pair_lanes(first, second, low):
    mixed = pltpu.roll(jnp.where(low, second, first), LANES // 2, axis=1)
    return jnp.where(low, first, mixed), jnp.where(low, mixed, second)


def slot_of(z, core, quad):
    turned = (z + DEPTH - CORES * core) % DEPTH
    inside = turned // QUAD == quad
    at = turned % QUAD
    return jnp.where(inside, at, QUAD - 1 - at), jnp.where(inside, 0, 1)


def right_side_kernel(
    spacing,
    piece,
    place_ref,
    degree_ref,
    same_ref,
    cross_ref,
    own_ref,
    own_forcing_ref,
    other_ref,
    other_forcing_ref,
    out_ref,
    state_buf,
    forcing_buf,
    out_buf,
    radial_buf,
    in_sem,
    out_sem,
):
    core, quad = place_ref[0], place_ref[1]
    chunks, _, fields, rows, cols = state_buf.shape
    whole = CORES * rows
    peers = out_buf.shape[0] // chunks

    def reads(i):
        columns = pl.ds(pl.multiple_of((CORES * i + core) * cols, cols), cols)
        pairs = [
            (own_ref, state_buf, core),
            (own_forcing_ref, forcing_buf, core),
            (other_ref, state_buf, 1 - core),
            (other_forcing_ref, forcing_buf, 1 - core),
        ]
        return [
            pltpu.make_async_copy(source.at[:, :, columns], target.at[i, which], in_sem.at[i, n])
            for n, (source, target, which) in enumerate(pairs)
        ]

    def write(i):
        block = pl.ds(i * peers, peers)
        return pltpu.make_async_copy(out_buf.at[block], out_ref.at[block], out_sem.at[i])

    for i in range(chunks):
        for copy in reads(i):
            copy.start()

    row = lax.broadcasted_iota(jnp.int32, (whole, LANES), 0)
    low = lax.broadcasted_iota(jnp.int32, (whole, LANES), 1) < piece
    first_row, last_row = row[:8] == 0, row[whole - 8 :] == whole - 1
    chip = lax.axis_index("rad") // CORES
    radius = R_INNER + spacing * (chip * whole + row).astype(jnp.float32)
    ratio = spacing / radius
    square = (spacing * spacing) / (radius * radius)
    for f, weight in enumerate(EXPLICIT_WEIGHT):
        radial_buf[f, 0] = weight * (1.0 + ratio)
        radial_buf[f, 1] = weight * (1.0 - ratio)
        radial_buf[f, 2] = weight * square

    @pl.loop(0, chunks)
    def _(i):
        for copy in reads(i):
            copy.wait()
        for j in range(cols // LANES):
            lanes = slice(j * LANES, (j + 1) * LANES)
            columns = pl.ds(
                pl.multiple_of((CORES * i + core) * cols + j * LANES, LANES), LANES
            )
            degree = jnp.where(
                low[:1], degree_ref[i, 2 * j : 2 * j + 1], degree_ref[i, 2 * j + 1 : 2 * j + 2]
            )
            term = degree * (degree + 1.0)
            sides = []
            for f, weight in enumerate(EXPLICIT_WEIGHT):
                same, cross = same_ref[f, :, columns], cross_ref[f, :, columns]
                above_edge = jnp.where(core == 0, same, cross)
                below_edge = jnp.where(core == 0, cross, same)
                values = jnp.concatenate([state_buf[i, c, f, :, lanes] for c in range(CORES)], axis=0)
                extra = jnp.concatenate(
                    [forcing_buf[i, c, f, :, lanes].astype(jnp.float32) for c in range(CORES)], axis=0
                )
                above = pltpu.roll(values, whole - 1, axis=0)
                below = pltpu.roll(values, 1, axis=0)
                above = jnp.concatenate(
                    [above[: whole - 8], jnp.where(last_row, above_edge, above[whole - 8 :])], axis=0
                )
                below = jnp.concatenate(
                    [jnp.where(first_row, below_edge, below[:8]), below[8:]], axis=0
                )
                sides.append(
                    values * ((1.0 - 2.0 * weight) - radial_buf[f, 2] * term)
                    + FORCING_STEP * extra
                    + above * radial_buf[f, 0]
                    + below * radial_buf[f, 1]
                )
            pieces = pair_lanes(*sides, low)
            half, pair = divmod(2 * j, DEPTH)
            for parity in range(2):
                at, slot = slot_of(pair + parity, core, quad)
                out_buf[i * peers + half * QUAD + at, slot] = (
                    pieces[parity].reshape(CORES, rows, LANES).astype(jnp.bfloat16)
                )
        write(i).start()

    for i in range(chunks):
        write(i).wait()


def solve_kernel(piece, own_ref, *refs):
    *mirror_refs, side_ref, out_ref = refs
    chips, groups, slots, cores, rows, _ = side_ref.shape
    whole = chips * cores * rows
    low = lax.broadcasted_iota(jnp.int32, (whole, groups * LANES), 1) % LANES < piece
    own = [own_ref[f, 0] for f in range(own_ref.shape[0])]
    mirror = [ref[0, 0] for ref in mirror_refs]
    for slot, inverse in enumerate((own, mirror)):
        side = jnp.concatenate(
            [
                side_ref[:, g, slot].astype(jnp.float32).reshape(whole, LANES).astype(jnp.bfloat16)
                for g in range(groups)
            ],
            axis=1,
        )
        solved = jnp.where(
            low,
            jnp.dot(inverse[0], side, preferred_element_type=jnp.float32),
            jnp.dot(inverse[1], side, preferred_element_type=jnp.float32),
        )
        for g in range(groups):
            out_ref[:, g, slot] = (
                solved[:, g * LANES : (g + 1) * LANES]
                .reshape(chips, cores, rows, LANES)
                .astype(jnp.bfloat16)
            )


def unpack_kernel(piece, turn, place_ref, solved_ref, *refs):
    out_ref, in_buf, out_buf, in_sem, out_sem = refs[-5:]
    here = place_ref[0]
    core = here if turn == 0 else 1 - here
    quad = place_ref[1 + turn]
    chunks, peers = in_buf.shape[:2]
    rows, cols = out_buf.shape[2:]
    low = lax.broadcasted_iota(jnp.int32, (rows, LANES), 1) < piece

    def read(i):
        return pltpu.make_async_copy(
            solved_ref.at[pl.ds(i * peers, peers), :, here], in_buf.at[i], in_sem.at[i]
        )

    def write(i):
        columns = pl.ds(pl.multiple_of((CORES * i + core) * cols, cols), cols)
        return pltpu.make_async_copy(out_buf.at[i], out_ref.at[:, :, columns], out_sem.at[i])

    for i in range(chunks):
        read(i).start()

    @pl.loop(0, chunks)
    def _(i):
        read(i).wait()
        for j in range(cols // LANES):
            lanes = slice(j * LANES, (j + 1) * LANES)
            half, pair = divmod(2 * j, DEPTH)
            parts = []
            for parity in range(2):
                at, slot = slot_of(pair + parity, core, quad)
                parts.append(in_buf[i, half * QUAD + at, slot].astype(jnp.float32))
            first, second = pair_lanes(*parts, low)
            out_buf[i, 0, :, lanes] = first.astype(jnp.bfloat16)
            out_buf[i, 1, :, lanes] = second.astype(jnp.bfloat16)
        write(i).start()

    for i in range(chunks):
        write(i).wait()


def body(field_state, forcing, inverses, owned_degree):
    fields, rows, group_cols = field_state.shape
    rad_count = lax.axis_size("rad")
    mode_count = lax.axis_size("mode")
    chips = rad_count // CORES
    spread = mode_count // DEPTH
    slots = rad_count * mode_count
    peers = chips * spread * QUAD
    whole_rows = rows * rad_count
    piece = group_cols // slots
    chip_cols = mode_count * piece
    core_cols = group_cols // CORES
    spacing = (R_OUTER - R_INNER) / (whole_rows - 1)

    def device(chip, core, x, z):
        return (chip * CORES + core) * mode_count + x * DEPTH + z

    quads = [
        [
            device(chip, core, x, (quad * QUAD + at + CORES * core) % DEPTH)
            for chip in range(chips)
            for x in range(spread)
            for at in range(QUAD)
        ]
        for core in range(CORES)
        for quad in range(DEPTH // QUAD)
    ]
    mirror = [
        (
            device(chip, core, x, (w + CORES * core) % DEPTH),
            device(chip, core, x, (DEPTH - 1 - w + CORES * core) % DEPTH),
        )
        for chip in range(chips)
        for core in range(CORES)
        for x in range(spread)
        for w in range(DEPTH)
    ]
    same_core = [[chip * CORES + core for chip in range(chips)] for core in range(CORES)]
    sibling = [(r, r ^ 1) for r in range(rad_count)]
    same_edge = [(r, r + 2) for r in range(1, rad_count - 2, 2)] + [
        (r, r - 2) for r in range(2, rad_count, 2)
    ]
    cross_edge = [(r, r + 1) for r in range(1, rad_count - 1, 2)] + [
        (r, r - 1) for r in range(2, rad_count, 2)
    ]

    core = lax.axis_index("rad") % CORES
    turned = [(lax.axis_index("mode") + DEPTH - CORES * c) % DEPTH for c in (core, 1 - core)]
    place = jnp.stack([core, turned[0] // QUAD, turned[1] // QUAD]).astype(jnp.int32)

    other_forcing = lax.ppermute(forcing, "rad", sibling)
    other_state = lax.ppermute(field_state, "rad", sibling)
    degree = jnp.broadcast_to(owned_degree.astype(jnp.float32)[:, None], (mode_count, LANES))
    degree = lax.all_to_all(degree, "mode", 0, 0, tiled=True)
    first_mirror = lax.ppermute(inverses[:1], AXES, mirror)
    edge = lax.dynamic_slice_in_dim(field_state, core * (rows - 1), 1, axis=1)
    same = lax.ppermute(edge, "rad", same_edge)
    cross = lax.ppermute(edge, "rad", cross_edge)
    degree, same, cross = lax.optimization_barrier((degree, same, cross))
    first_mirror, second_inverse, degree = lax.optimization_barrier(
        (first_mirror, inverses[1:], degree)
    )
    second_mirror = lax.ppermute(second_inverse, AXES, mirror)
    degree = jnp.broadcast_to(degree[None], (chips, mode_count, LANES))
    degree = lax.all_to_all(degree, "rad", 0, 0, axis_index_groups=same_core, tiled=True)

    anywhere = pl.BlockSpec(memory_space=pl.ANY)
    vmem = pl.BlockSpec(memory_space=pltpu.VMEM)
    smem = pl.BlockSpec(memory_space=pltpu.SMEM)
    packed = pl.pallas_call(
        functools.partial(right_side_kernel, spacing, piece),
        in_specs=[smem, vmem, vmem, vmem, anywhere, anywhere, anywhere, anywhere],
        out_specs=anywhere,
        out_shape=jax.ShapeDtypeStruct((peers, 2, CORES, rows, LANES), jnp.bfloat16),
        scratch_shapes=[
            pltpu.VMEM((chips, CORES, fields, rows, chip_cols), jnp.float32),
            pltpu.VMEM((chips, CORES, fields, rows, chip_cols), jnp.bfloat16),
            pltpu.VMEM((peers, 2, CORES, rows, LANES), jnp.bfloat16),
            pltpu.VMEM((fields, 3, CORES * rows, LANES), jnp.float32),
            pltpu.SemaphoreType.DMA((chips, 4)),
            pltpu.SemaphoreType.DMA((chips,)),
        ],
        compiler_params=pltpu.CompilerParams(vmem_limit_bytes=LARGE_VMEM),
        name="right_side",
    )(place, degree, same, cross, field_state, forcing, other_state, other_forcing)

    packed, second_mirror = lax.optimization_barrier((packed, second_mirror))
    packed = lax.all_to_all(packed, AXES, 0, 0, axis_index_groups=quads, tiled=True)

    groups = 2
    grouped = (chips, spread * QUAD, 2, CORES, rows, LANES)
    block = pl.BlockSpec((chips, groups, 2, CORES, rows, LANES), lambda i: (0, i, 0, 0, 0, 0))
    own_block = pl.BlockSpec((fields, 1, whole_rows, whole_rows), lambda i: (0, 0, 0, 0))
    mirror_block = pl.BlockSpec((1, 1, whole_rows, whole_rows), lambda i: (0, 0, 0, 0))
    solved = pl.pallas_call(
        functools.partial(solve_kernel, piece),
        grid=(spread * QUAD // groups,),
        in_specs=[own_block, mirror_block, mirror_block, block],
        out_specs=block,
        out_shape=jax.ShapeDtypeStruct(grouped, jnp.bfloat16),
        compiler_params=pltpu.CompilerParams(vmem_limit_bytes=SMALL_VMEM),
        name="solve",
    )(inverses, first_mirror, second_mirror, packed.reshape(grouped))

    solved = lax.all_to_all(
        solved.reshape(peers, 2, CORES, rows, LANES),
        AXES,
        0,
        0,
        axis_index_groups=quads,
        tiled=True,
    )

    def unpack(turn, solved, *partial):
        return pl.pallas_call(
            functools.partial(unpack_kernel, piece, turn),
            in_specs=[smem, anywhere] + [anywhere] * len(partial),
            out_specs=anywhere,
            out_shape=jax.ShapeDtypeStruct((fields, rows, group_cols), jnp.bfloat16),
            scratch_shapes=[
                pltpu.VMEM((chips, spread * QUAD, 2, rows, LANES), jnp.bfloat16),
                pltpu.VMEM((chips, fields, rows, chip_cols), jnp.bfloat16),
                pltpu.SemaphoreType.DMA((chips,)),
                pltpu.SemaphoreType.DMA((chips,)),
            ],
            input_output_aliases={2: 0} if partial else {},
            compiler_params=pltpu.CompilerParams(vmem_limit_bytes=SMALL_VMEM),
            cost_estimate=pl.CostEstimate(
                flops=2 * field_state.size, bytes_accessed=2 * field_state.size, transcendentals=0
            ),
            name="unpack_other" if turn else "unpack_own",
        )(place, solved, *partial)

    returned = lax.ppermute(solved, "rad", sibling)
    partial = unpack(0, solved)
    return unpack(1, returned, partial)


def solution(mesh):
    in_specs = (
        P(None, "rad", "mode"),
        P(None, "rad", "mode"),
        P(None, ("rad", "mode"), None, None),
        P(("rad", "mode")),
    )
    out_specs = P(None, "rad", "mode")
    return jax.shard_map(body, mesh=mesh, in_specs=in_specs, out_specs=out_specs, check_vma=False)
```

```python
import functools

import jax
import jax.numpy as jnp
from jax import lax
from jax.experimental import pallas as pl
from jax.experimental.pallas import tpu as pltpu
from jax.sharding import PartitionSpec as P

R_INNER = 0.35
R_OUTER = 1.0
EXPLICIT_WEIGHT = (0.45, 0.35)
FORCING_STEP = 0.5
AXES = ("rad", "mode")
LANES = 128
CORES = 2
DEPTH = 8
QUAD = DEPTH // 2
AHEAD = 3
SMALL_VMEM = 24 * 1024 * 1024
LARGE_VMEM = 56 * 1024 * 1024


def pair_lanes(first, second, low):
    mixed = pltpu.roll(jnp.where(low, second, first), LANES // 2, axis=1)
    return jnp.where(low, first, mixed), jnp.where(low, mixed, second)


def slot_of(z, core, quad):
    turned = (z + DEPTH - CORES * core) % DEPTH
    inside = turned // QUAD == quad
    at = turned % QUAD
    return jnp.where(inside, at, QUAD - 1 - at), jnp.where(inside, 0, 1)


def right_side_kernel(
    spacing,
    piece,
    place_ref,
    degree_ref,
    same_ref,
    cross_ref,
    own_ref,
    own_forcing_ref,
    other_ref,
    other_forcing_ref,
    out_ref,
    state_buf,
    forcing_buf,
    out_buf,
    radial_buf,
    in_sem,
    out_sem,
):
    core, quad = place_ref[0], place_ref[1]
    chunks, _, fields, rows, cols = state_buf.shape
    whole = CORES * rows
    peers = out_buf.shape[0] // chunks

    def reads(i):
        columns = pl.ds(pl.multiple_of((CORES * i + core) * cols, cols), cols)
        pairs = [
            (own_ref, state_buf, core),
            (own_forcing_ref, forcing_buf, core),
            (other_ref, state_buf, 1 - core),
            (other_forcing_ref, forcing_buf, 1 - core),
        ]
        return [
            pltpu.make_async_copy(source.at[:, :, columns], target.at[i, which], in_sem.at[i, n])
            for n, (source, target, which) in enumerate(pairs)
        ]

    def write(i):
        block = pl.ds(i * peers, peers)
        return pltpu.make_async_copy(out_buf.at[block], out_ref.at[block], out_sem.at[i])

    for i in range(AHEAD):
        for copy in reads(i):
            copy.start()

    row = lax.broadcasted_iota(jnp.int32, (whole, LANES), 0)
    low = lax.broadcasted_iota(jnp.int32, (whole, LANES), 1) < piece
    first_row, last_row = row[:8] == 0, row[whole - 8 :] == whole - 1
    chip = lax.axis_index("rad") // CORES
    radius = R_INNER + spacing * (chip * whole + row).astype(jnp.float32)
    ratio = spacing / radius
    square = (spacing * spacing) / (radius * radius)
    for f, weight in enumerate(EXPLICIT_WEIGHT):
        radial_buf[f, 0] = weight * (1.0 + ratio)
        radial_buf[f, 1] = weight * (1.0 - ratio)
        radial_buf[f, 2] = weight * square

    @pl.loop(0, chunks)
    def _(i):
        @pl.when(i + AHEAD < chunks)
        def _():
            for copy in reads(i + AHEAD):
                copy.start()

        for copy in reads(i):
            copy.wait()
        for j in range(cols // LANES):
            lanes = slice(j * LANES, (j + 1) * LANES)
            columns = pl.ds(
                pl.multiple_of((CORES * i + core) * cols + j * LANES, LANES), LANES
            )
            degree = jnp.where(
                low[:1], degree_ref[i, 2 * j : 2 * j + 1], degree_ref[i, 2 * j + 1 : 2 * j + 2]
            )
            term = degree * (degree + 1.0)
            sides = []
            for f, weight in enumerate(EXPLICIT_WEIGHT):
                same, cross = same_ref[f, :, columns], cross_ref[f, :, columns]
                above_edge = jnp.where(core == 0, same, cross)
                below_edge = jnp.where(core == 0, cross, same)
                values = jnp.concatenate([state_buf[i, c, f, :, lanes] for c in range(CORES)], axis=0)
                extra = jnp.concatenate(
                    [forcing_buf[i, c, f, :, lanes].astype(jnp.float32) for c in range(CORES)], axis=0
                )
                above = pltpu.roll(values, whole - 1, axis=0)
                below = pltpu.roll(values, 1, axis=0)
                above = jnp.concatenate(
                    [above[: whole - 8], jnp.where(last_row, above_edge, above[whole - 8 :])], axis=0
                )
                below = jnp.concatenate(
                    [jnp.where(first_row, below_edge, below[:8]), below[8:]], axis=0
                )
                sides.append(
                    values * ((1.0 - 2.0 * weight) - radial_buf[f, 2] * term)
                    + FORCING_STEP * extra
                    + above * radial_buf[f, 0]
                    + below * radial_buf[f, 1]
                )
            pieces = pair_lanes(*sides, low)
            half, pair = divmod(2 * j, DEPTH)
            for parity in range(2):
                at, slot = slot_of(pair + parity, core, quad)
                out_buf[i * peers + half * QUAD + at, slot] = (
                    pieces[parity].reshape(CORES, rows, LANES).astype(jnp.bfloat16)
                )
        write(i).start()

    for i in range(chunks):
        write(i).wait()


def solve_kernel(piece, own_ref, *refs):
    *mirror_refs, side_ref, out_ref = refs
    chips, groups, slots, cores, rows, _ = side_ref.shape
    whole = chips * cores * rows
    low = lax.broadcasted_iota(jnp.int32, (whole, LANES), 1) < piece
    own = [own_ref[f, 0] for f in range(own_ref.shape[0])]
    mirror = [ref[0, 0] for ref in mirror_refs]
    for slot, inverse in enumerate((own, mirror)):
        pairs = []
        for g in range(0, groups, 2):
            packed = [
                side_ref[:, g + n, slot].astype(jnp.float32).reshape(whole, LANES) for n in range(2)
            ]
            pairs.append(pair_lanes(*packed, low))
        solved = [
            jnp.dot(
                inverse[f],
                jnp.concatenate([pair[f].astype(jnp.bfloat16) for pair in pairs], axis=1),
                preferred_element_type=jnp.float32,
            )
            for f in range(2)
        ]
        for g in range(0, groups, 2):
            lanes = slice(g // 2 * LANES, (g // 2 + 1) * LANES)
            packed = pair_lanes(solved[0][:, lanes], solved[1][:, lanes], low)
            for n in range(2):
                out_ref[:, g + n, slot] = (
                    packed[n].reshape(chips, cores, rows, LANES).astype(jnp.bfloat16)
                )


def unpack_kernel(piece, turn, place_ref, solved_ref, *refs):
    out_ref, in_buf, out_buf, in_sem, out_sem = refs[-5:]
    here = place_ref[0]
    core = here if turn == 0 else 1 - here
    quad = place_ref[1 + turn]
    chunks, peers = in_buf.shape[:2]
    rows, cols = out_buf.shape[2:]
    low = lax.broadcasted_iota(jnp.int32, (rows, LANES), 1) < piece

    def read(i):
        return pltpu.make_async_copy(
            solved_ref.at[pl.ds(i * peers, peers), :, here], in_buf.at[i], in_sem.at[i]
        )

    def write(i):
        columns = pl.ds(pl.multiple_of((CORES * i + core) * cols, cols), cols)
        return pltpu.make_async_copy(out_buf.at[i], out_ref.at[:, :, columns], out_sem.at[i])

    for i in range(chunks):
        read(i).start()

    @pl.loop(0, chunks)
    def _(i):
        read(i).wait()
        for j in range(cols // LANES):
            lanes = slice(j * LANES, (j + 1) * LANES)
            half, pair = divmod(2 * j, DEPTH)
            parts = []
            for parity in range(2):
                at, slot = slot_of(pair + parity, core, quad)
                parts.append(in_buf[i, half * QUAD + at, slot].astype(jnp.float32))
            first, second = pair_lanes(*parts, low)
            out_buf[i, 0, :, lanes] = first.astype(jnp.bfloat16)
            out_buf[i, 1, :, lanes] = second.astype(jnp.bfloat16)
        write(i).start()

    for i in range(chunks):
        write(i).wait()


def body(field_state, forcing, inverses, owned_degree):
    fields, rows, group_cols = field_state.shape
    rad_count = lax.axis_size("rad")
    mode_count = lax.axis_size("mode")
    chips = rad_count // CORES
    spread = mode_count // DEPTH
    slots = rad_count * mode_count
    peers = chips * spread * QUAD
    whole_rows = rows * rad_count
    piece = group_cols // slots
    chip_cols = mode_count * piece
    core_cols = group_cols // CORES
    spacing = (R_OUTER - R_INNER) / (whole_rows - 1)

    def device(chip, core, x, z):
        return (chip * CORES + core) * mode_count + x * DEPTH + z

    quads = [
        [
            device(chip, core, x, (quad * QUAD + at + CORES * core) % DEPTH)
            for chip in range(chips)
            for x in range(spread)
            for at in range(QUAD)
        ]
        for core in range(CORES)
        for quad in range(DEPTH // QUAD)
    ]
    mirror = [
        (
            device(chip, core, x, (w + CORES * core) % DEPTH),
            device(chip, core, x, (DEPTH - 1 - w + CORES * core) % DEPTH),
        )
        for chip in range(chips)
        for core in range(CORES)
        for x in range(spread)
        for w in range(DEPTH)
    ]
    same_core = [[chip * CORES + core for chip in range(chips)] for core in range(CORES)]
    sibling = [(r, r ^ 1) for r in range(rad_count)]
    same_edge = [(r, r + 2) for r in range(1, rad_count - 2, 2)] + [
        (r, r - 2) for r in range(2, rad_count, 2)
    ]
    cross_edge = [(r, r + 1) for r in range(1, rad_count - 1, 2)] + [
        (r, r - 1) for r in range(2, rad_count, 2)
    ]

    core = lax.axis_index("rad") % CORES
    turned = [(lax.axis_index("mode") + DEPTH - CORES * c) % DEPTH for c in (core, 1 - core)]
    place = jnp.stack([core, turned[0] // QUAD, turned[1] // QUAD]).astype(jnp.int32)

    other_forcing = lax.ppermute(forcing, "rad", sibling)
    other_state = lax.ppermute(field_state, "rad", sibling)
    degree = jnp.broadcast_to(owned_degree.astype(jnp.float32)[:, None], (mode_count, LANES))
    degree = lax.all_to_all(degree, "mode", 0, 0, tiled=True)
    first_mirror = lax.ppermute(inverses[:1], AXES, mirror)
    edge = lax.dynamic_slice_in_dim(field_state, core * (rows - 1), 1, axis=1)
    same = lax.ppermute(edge, "rad", same_edge)
    cross = lax.ppermute(edge, "rad", cross_edge)
    degree, same, cross = lax.optimization_barrier((degree, same, cross))
    first_mirror, second_inverse, degree = lax.optimization_barrier(
        (first_mirror, inverses[1:], degree)
    )
    second_mirror = lax.ppermute(second_inverse, AXES, mirror)
    degree = jnp.broadcast_to(degree[None], (chips, mode_count, LANES))
    degree = lax.all_to_all(degree, "rad", 0, 0, axis_index_groups=same_core, tiled=True)

    anywhere = pl.BlockSpec(memory_space=pl.ANY)
    vmem = pl.BlockSpec(memory_space=pltpu.VMEM)
    smem = pl.BlockSpec(memory_space=pltpu.SMEM)
    packed = pl.pallas_call(
        functools.partial(right_side_kernel, spacing, piece),
        in_specs=[smem, vmem, vmem, vmem, anywhere, anywhere, anywhere, anywhere],
        out_specs=anywhere,
        out_shape=jax.ShapeDtypeStruct((peers, 2, CORES, rows, LANES), jnp.bfloat16),
        scratch_shapes=[
            pltpu.VMEM((chips, CORES, fields, rows, chip_cols), jnp.float32),
            pltpu.VMEM((chips, CORES, fields, rows, chip_cols), jnp.bfloat16),
            pltpu.VMEM((peers, 2, CORES, rows, LANES), jnp.bfloat16),
            pltpu.VMEM((fields, 3, CORES * rows, LANES), jnp.float32),
            pltpu.SemaphoreType.DMA((chips, 4)),
            pltpu.SemaphoreType.DMA((chips,)),
        ],
        compiler_params=pltpu.CompilerParams(vmem_limit_bytes=LARGE_VMEM),
        name="right_side",
    )(place, degree, same, cross, field_state, forcing, other_state, other_forcing)

    packed, second_mirror = lax.optimization_barrier((packed, second_mirror))
    packed = lax.all_to_all(packed, AXES, 0, 0, axis_index_groups=quads, tiled=True)

    groups = 4
    grouped = (chips, spread * QUAD, 2, CORES, rows, LANES)
    block = pl.BlockSpec((chips, groups, 2, CORES, rows, LANES), lambda i: (0, i, 0, 0, 0, 0))
    own_block = pl.BlockSpec((fields, 1, whole_rows, whole_rows), lambda i: (0, 0, 0, 0))
    mirror_block = pl.BlockSpec((1, 1, whole_rows, whole_rows), lambda i: (0, 0, 0, 0))
    solved = pl.pallas_call(
        functools.partial(solve_kernel, piece),
        grid=(spread * QUAD // groups,),
        in_specs=[own_block, mirror_block, mirror_block, block],
        out_specs=block,
        out_shape=jax.ShapeDtypeStruct(grouped, jnp.bfloat16),
        compiler_params=pltpu.CompilerParams(vmem_limit_bytes=SMALL_VMEM),
        name="solve",
    )(inverses, first_mirror, second_mirror, packed.reshape(grouped))

    solved = lax.all_to_all(
        solved.reshape(peers, 2, CORES, rows, LANES),
        AXES,
        0,
        0,
        axis_index_groups=quads,
        tiled=True,
    )

    def unpack(turn, solved, *partial):
        return pl.pallas_call(
            functools.partial(unpack_kernel, piece, turn),
            in_specs=[smem, anywhere] + [anywhere] * len(partial),
            out_specs=anywhere,
            out_shape=jax.ShapeDtypeStruct((fields, rows, group_cols), jnp.bfloat16),
            scratch_shapes=[
                pltpu.VMEM((chips, spread * QUAD, 2, rows, LANES), jnp.bfloat16),
                pltpu.VMEM((chips, fields, rows, chip_cols), jnp.bfloat16),
                pltpu.SemaphoreType.DMA((chips,)),
                pltpu.SemaphoreType.DMA((chips,)),
            ],
            input_output_aliases={2: 0} if partial else {},
            compiler_params=pltpu.CompilerParams(vmem_limit_bytes=SMALL_VMEM),
            cost_estimate=pl.CostEstimate(
                flops=2 * field_state.size, bytes_accessed=2 * field_state.size, transcendentals=0
            ),
            name="unpack_other" if turn else "unpack_own",
        )(place, solved, *partial)

    returned = lax.ppermute(solved, "rad", sibling)
    partial = unpack(0, solved)
    return unpack(1, returned, partial)


def solution(mesh):
    in_specs = (
        P(None, "rad", "mode"),
        P(None, "rad", "mode"),
        P(None, ("rad", "mode"), None, None),
        P(("rad", "mode")),
    )
    out_specs = P(None, "rad", "mode")
    return jax.shard_map(body, mesh=mesh, in_specs=in_specs, out_specs=out_specs, check_vma=False)
```

```python
import functools

import jax
import jax.numpy as jnp
from jax import lax
from jax.experimental import pallas as pl
from jax.experimental.pallas import tpu as pltpu
from jax.sharding import PartitionSpec as P

R_INNER = 0.35
R_OUTER = 1.0
EXPLICIT_WEIGHT = (0.45, 0.35)
FORCING_STEP = 0.5
AXES = ("rad", "mode")
LANES = 128
CORES = 2
DEPTH = 8
QUAD = DEPTH // 2
AHEAD = 3
SMALL_VMEM = 24 * 1024 * 1024
LARGE_VMEM = 56 * 1024 * 1024


def pair_lanes(first, second, low):
    mixed = pltpu.roll(jnp.where(low, second, first), LANES // 2, axis=1)
    return jnp.where(low, first, mixed), jnp.where(low, mixed, second)


def slot_of(z, core, quad):
    turned = (z + DEPTH - CORES * core) % DEPTH
    inside = turned // QUAD == quad
    at = turned % QUAD
    return jnp.where(inside, at, QUAD - 1 - at), jnp.where(inside, 0, 1)


def right_side_kernel(
    spacing,
    piece,
    place_ref,
    degree_ref,
    same_ref,
    cross_ref,
    own_ref,
    own_forcing_ref,
    other_ref,
    other_forcing_ref,
    out_ref,
    state_buf,
    forcing_buf,
    out_buf,
    radial_buf,
    in_sem,
    out_sem,
):
    core, quad = place_ref[0], place_ref[1]
    chunks, _, fields, rows, cols = state_buf.shape
    whole = CORES * rows
    peers = out_buf.shape[0] // chunks

    def reads(i):
        columns = pl.ds(pl.multiple_of((CORES * i + core) * cols, cols), cols)
        pairs = [
            (own_ref, state_buf, core),
            (own_forcing_ref, forcing_buf, core),
            (other_ref, state_buf, 1 - core),
            (other_forcing_ref, forcing_buf, 1 - core),
        ]
        return [
            pltpu.make_async_copy(source.at[:, :, columns], target.at[i, which], in_sem.at[i, n])
            for n, (source, target, which) in enumerate(pairs)
        ]

    def write(i):
        block = pl.ds(i * peers, peers)
        return pltpu.make_async_copy(out_buf.at[block], out_ref.at[block], out_sem.at[i])

    for i in range(AHEAD):
        for copy in reads(i):
            copy.start()

    row = lax.broadcasted_iota(jnp.int32, (whole, LANES), 0)
    low = lax.broadcasted_iota(jnp.int32, (whole, LANES), 1) < piece
    first_row, last_row = row[:8] == 0, row[whole - 8 :] == whole - 1
    chip = lax.axis_index("rad") // CORES
    radius = R_INNER + spacing * (chip * whole + row).astype(jnp.float32)
    ratio = spacing / radius
    square = (spacing * spacing) / (radius * radius)
    for f, weight in enumerate(EXPLICIT_WEIGHT):
        radial_buf[f, 0] = weight * (1.0 + ratio)
        radial_buf[f, 1] = weight * (1.0 - ratio)
        radial_buf[f, 2] = weight * square

    @pl.loop(0, chunks)
    def _(i):
        @pl.when(i + AHEAD < chunks)
        def _():
            for copy in reads(i + AHEAD):
                copy.start()

        for copy in reads(i):
            copy.wait()
        for j in range(cols // LANES):
            lanes = slice(j * LANES, (j + 1) * LANES)
            columns = pl.ds(
                pl.multiple_of((CORES * i + core) * cols + j * LANES, LANES), LANES
            )
            degree = jnp.where(
                low[:1], degree_ref[i, 2 * j : 2 * j + 1], degree_ref[i, 2 * j + 1 : 2 * j + 2]
            )
            term = degree * (degree + 1.0)
            sides = []
            for f, weight in enumerate(EXPLICIT_WEIGHT):
                same, cross = same_ref[f, :, columns], cross_ref[f, :, columns]
                above_edge = jnp.where(core == 0, same, cross)
                below_edge = jnp.where(core == 0, cross, same)
                values = jnp.concatenate([state_buf[i, c, f, :, lanes] for c in range(CORES)], axis=0)
                extra = jnp.concatenate(
                    [forcing_buf[i, c, f, :, lanes].astype(jnp.float32) for c in range(CORES)], axis=0
                )
                above = pltpu.roll(values, whole - 1, axis=0)
                below = pltpu.roll(values, 1, axis=0)
                above = jnp.concatenate(
                    [above[: whole - 8], jnp.where(last_row, above_edge, above[whole - 8 :])], axis=0
                )
                below = jnp.concatenate(
                    [jnp.where(first_row, below_edge, below[:8]), below[8:]], axis=0
                )
                sides.append(
                    values * ((1.0 - 2.0 * weight) - radial_buf[f, 2] * term)
                    + FORCING_STEP * extra
                    + above * radial_buf[f, 0]
                    + below * radial_buf[f, 1]
                )
            pieces = pair_lanes(*sides, low)
            half, pair = divmod(2 * j, DEPTH)
            for parity in range(2):
                at, slot = slot_of(pair + parity, core, quad)
                out_buf[i * peers + half * QUAD + at, slot] = (
                    pieces[parity].reshape(CORES, rows, LANES).astype(jnp.bfloat16)
                )
        write(i).start()

    for i in range(chunks):
        write(i).wait()


def solve_kernel(piece, own_ref, *refs):
    *mirror_refs, side_ref, out_ref = refs
    chips, groups, slots, cores, rows, _ = side_ref.shape
    whole = chips * cores * rows
    low = lax.broadcasted_iota(jnp.int32, (whole, LANES), 1) < piece
    for slot, parts in enumerate(([own_ref], mirror_refs)):
        pairs = []
        for g in range(0, groups, 2):
            packed = [
                side_ref[:, g + n, slot].astype(jnp.float32).reshape(whole, LANES) for n in range(2)
            ]
            pairs.append(pair_lanes(*packed, low))
        sides = [
            jnp.concatenate([pair[f].astype(jnp.bfloat16) for pair in pairs], axis=1)
            for f in range(2)
        ]
        solved = [
            jnp.concatenate(
                [
                    jnp.dot(part[f, 0], sides[f], preferred_element_type=jnp.float32)
                    for part in parts
                ],
                axis=0,
            )
            for f in range(2)
        ]
        for g in range(0, groups, 2):
            lanes = slice(g // 2 * LANES, (g // 2 + 1) * LANES)
            packed = pair_lanes(solved[0][:, lanes], solved[1][:, lanes], low)
            for n in range(2):
                out_ref[:, g + n, slot] = (
                    packed[n].reshape(chips, cores, rows, LANES).astype(jnp.bfloat16)
                )


def unpack_kernel(piece, turn, place_ref, solved_ref, *refs):
    out_ref, in_buf, out_buf, in_sem, out_sem = refs[-5:]
    here = place_ref[0]
    core = here if turn == 0 else 1 - here
    quad = place_ref[1 + turn]
    chunks, peers = in_buf.shape[:2]
    rows, cols = out_buf.shape[2:]
    low = lax.broadcasted_iota(jnp.int32, (rows, LANES), 1) < piece

    def read(i):
        return pltpu.make_async_copy(
            solved_ref.at[pl.ds(i * peers, peers), :, here], in_buf.at[i], in_sem.at[i]
        )

    def write(i):
        columns = pl.ds(pl.multiple_of((CORES * i + core) * cols, cols), cols)
        return pltpu.make_async_copy(out_buf.at[i], out_ref.at[:, :, columns], out_sem.at[i])

    for i in range(chunks):
        read(i).start()

    @pl.loop(0, chunks)
    def _(i):
        read(i).wait()
        for j in range(cols // LANES):
            lanes = slice(j * LANES, (j + 1) * LANES)
            half, pair = divmod(2 * j, DEPTH)
            parts = []
            for parity in range(2):
                at, slot = slot_of(pair + parity, core, quad)
                parts.append(in_buf[i, half * QUAD + at, slot].astype(jnp.float32))
            first, second = pair_lanes(*parts, low)
            out_buf[i, 0, :, lanes] = first.astype(jnp.bfloat16)
            out_buf[i, 1, :, lanes] = second.astype(jnp.bfloat16)
        write(i).start()

    for i in range(chunks):
        write(i).wait()


def body(field_state, forcing, inverses, owned_degree):
    fields, rows, group_cols = field_state.shape
    rad_count = lax.axis_size("rad")
    mode_count = lax.axis_size("mode")
    chips = rad_count // CORES
    spread = mode_count // DEPTH
    slots = rad_count * mode_count
    peers = chips * spread * QUAD
    whole_rows = rows * rad_count
    piece = group_cols // slots
    chip_cols = mode_count * piece
    core_cols = group_cols // CORES
    spacing = (R_OUTER - R_INNER) / (whole_rows - 1)

    def device(chip, core, x, z):
        return (chip * CORES + core) * mode_count + x * DEPTH + z

    quads = [
        [
            device(chip, core, x, (quad * QUAD + at + CORES * core) % DEPTH)
            for chip in range(chips)
            for x in range(spread)
            for at in range(QUAD)
        ]
        for core in range(CORES)
        for quad in range(DEPTH // QUAD)
    ]
    mirror = [
        (
            device(chip, core, x, (w + CORES * core) % DEPTH),
            device(chip, core, x, (DEPTH - 1 - w + CORES * core) % DEPTH),
        )
        for chip in range(chips)
        for core in range(CORES)
        for x in range(spread)
        for w in range(DEPTH)
    ]
    same_core = [[chip * CORES + core for chip in range(chips)] for core in range(CORES)]
    sibling = [(r, r ^ 1) for r in range(rad_count)]
    same_edge = [(r, r + 2) for r in range(1, rad_count - 2, 2)] + [
        (r, r - 2) for r in range(2, rad_count, 2)
    ]
    cross_edge = [(r, r + 1) for r in range(1, rad_count - 1, 2)] + [
        (r, r - 1) for r in range(2, rad_count, 2)
    ]

    core = lax.axis_index("rad") % CORES
    turned = [(lax.axis_index("mode") + DEPTH - CORES * c) % DEPTH for c in (core, 1 - core)]
    place = jnp.stack([core, turned[0] // QUAD, turned[1] // QUAD]).astype(jnp.int32)

    early = whole_rows // 2
    other_forcing = lax.ppermute(forcing, "rad", sibling)
    other_state = lax.ppermute(field_state, "rad", sibling)
    degree = jnp.broadcast_to(owned_degree.astype(jnp.float32)[:, None], (mode_count, LANES))
    degree = lax.all_to_all(degree, "mode", 0, 0, tiled=True)
    first_mirror = lax.ppermute(inverses[:, :, :early], AXES, mirror)
    edge = lax.dynamic_slice_in_dim(field_state, core * (rows - 1), 1, axis=1)
    same = lax.ppermute(edge, "rad", same_edge)
    cross = lax.ppermute(edge, "rad", cross_edge)
    degree, same, cross = lax.optimization_barrier((degree, same, cross))
    first_mirror, second_inverse, degree = lax.optimization_barrier(
        (first_mirror, inverses[:, :, early:], degree)
    )
    second_mirror = lax.ppermute(second_inverse, AXES, mirror)
    degree = jnp.broadcast_to(degree[None], (chips, mode_count, LANES))
    degree = lax.all_to_all(degree, "rad", 0, 0, axis_index_groups=same_core, tiled=True)

    anywhere = pl.BlockSpec(memory_space=pl.ANY)
    vmem = pl.BlockSpec(memory_space=pltpu.VMEM)
    smem = pl.BlockSpec(memory_space=pltpu.SMEM)
    packed = pl.pallas_call(
        functools.partial(right_side_kernel, spacing, piece),
        in_specs=[smem, vmem, vmem, vmem, anywhere, anywhere, anywhere, anywhere],
        out_specs=anywhere,
        out_shape=jax.ShapeDtypeStruct((peers, 2, CORES, rows, LANES), jnp.bfloat16),
        scratch_shapes=[
            pltpu.VMEM((chips, CORES, fields, rows, chip_cols), jnp.float32),
            pltpu.VMEM((chips, CORES, fields, rows, chip_cols), jnp.bfloat16),
            pltpu.VMEM((peers, 2, CORES, rows, LANES), jnp.bfloat16),
            pltpu.VMEM((fields, 3, CORES * rows, LANES), jnp.float32),
            pltpu.SemaphoreType.DMA((chips, 4)),
            pltpu.SemaphoreType.DMA((chips,)),
        ],
        compiler_params=pltpu.CompilerParams(vmem_limit_bytes=LARGE_VMEM),
        name="right_side",
    )(place, degree, same, cross, field_state, forcing, other_state, other_forcing)

    packed, second_mirror = lax.optimization_barrier((packed, second_mirror))
    packed = lax.all_to_all(packed, AXES, 0, 0, axis_index_groups=quads, tiled=True)

    groups = 4
    grouped = (chips, spread * QUAD, 2, CORES, rows, LANES)
    block = pl.BlockSpec((chips, groups, 2, CORES, rows, LANES), lambda i: (0, i, 0, 0, 0, 0))
    own_block = pl.BlockSpec((fields, 1, whole_rows, whole_rows), lambda i: (0, 0, 0, 0))
    mirror_blocks = [
        pl.BlockSpec((fields, 1, height, whole_rows), lambda i: (0, 0, 0, 0))
        for height in (early, whole_rows - early)
    ]
    solved = pl.pallas_call(
        functools.partial(solve_kernel, piece),
        grid=(spread * QUAD // groups,),
        in_specs=[own_block, *mirror_blocks, block],
        out_specs=block,
        out_shape=jax.ShapeDtypeStruct(grouped, jnp.bfloat16),
        compiler_params=pltpu.CompilerParams(vmem_limit_bytes=SMALL_VMEM),
        name="solve",
    )(inverses, first_mirror, second_mirror, packed.reshape(grouped))

    solved = lax.all_to_all(
        solved.reshape(peers, 2, CORES, rows, LANES),
        AXES,
        0,
        0,
        axis_index_groups=quads,
        tiled=True,
    )

    def unpack(turn, solved, *partial):
        return pl.pallas_call(
            functools.partial(unpack_kernel, piece, turn),
            in_specs=[smem, anywhere] + [anywhere] * len(partial),
            out_specs=anywhere,
            out_shape=jax.ShapeDtypeStruct((fields, rows, group_cols), jnp.bfloat16),
            scratch_shapes=[
                pltpu.VMEM((chips, spread * QUAD, 2, rows, LANES), jnp.bfloat16),
                pltpu.VMEM((chips, fields, rows, chip_cols), jnp.bfloat16),
                pltpu.SemaphoreType.DMA((chips,)),
                pltpu.SemaphoreType.DMA((chips,)),
            ],
            input_output_aliases={2: 0} if partial else {},
            compiler_params=pltpu.CompilerParams(vmem_limit_bytes=SMALL_VMEM),
            cost_estimate=pl.CostEstimate(
                flops=2 * field_state.size, bytes_accessed=2 * field_state.size, transcendentals=0
            ),
            name="unpack_other" if turn else "unpack_own",
        )(place, solved, *partial)

    returned = lax.ppermute(solved, "rad", sibling)
    partial = unpack(0, solved)
    return unpack(1, returned, partial)


def solution(mesh):
    in_specs = (
        P(None, "rad", "mode"),
        P(None, "rad", "mode"),
        P(None, ("rad", "mode"), None, None),
        P(("rad", "mode")),
    )
    out_specs = P(None, "rad", "mode")
    return jax.shard_map(body, mesh=mesh, in_specs=in_specs, out_specs=out_specs, check_vma=False)
```
